512 devices in a mesh: depth: 32 (over y, z_hi), xline: 16 (over x, z_lo, core).
Axes of the slice: x: 4, y: 8, z: 8 (z_hi: 4, z_lo: 2; z = z_hi * 2 + z_lo), core: 2. Of those that a mesh axis runs over, the one named last changes fastest.
Arguments:
- surface_fields: float32 [2, 2, 2, 256, 128], P(None, None, None, 'xline'), may hold values from -6 to 6
- stencil_table: float32 [13, 2, 2, 128], replicated
- velocity_bins: int32 [32, 2, 256, 128], P('depth', None, 'xline'), may hold values from 0 to 127
- offset_list: int32 [16, 2], replicated, may hold values from -8 to 8, as said below
Outputs:
- image_tiles: float32 [32, 16, 256, 128], P('depth', None, 'xline')
The draws below stay inside these ranges and needn't reach their ends.
Inputs may be any that keep to these rules, and one draw needn't show every extreme that they name: `offset_list`: column 0 lies within -8 to 8 and column 1 within -8 to 8; both ends of both ranges occur in every draw.
All inputs are finite; a program needn't handle non-finite values.
Results may differ from the reference program's by a relative error of at most 0.0003.
Values sent between devices are 32-bit elements; how exact they have to be, the bound alone decides.
A program may use at most 64 MiB of HBM per device.

```python
import jax
import jax.numpy as jnp
from jax import lax

NXI = 128
F = 2
LEVELS = 2
TAPS = 13
NVEL = 128
OFFS = 16
OFF_Y = 8
OFF_X = 8
SLABS = 32
CROSS = 256


def draw_stencil_table(key, part):
    subkeys = jax.random.split(key, 5)
    share_freq = 0.1 * 2.5 ** jax.random.uniform(subkeys[0], (F,))
    bin_ids = jnp.arange(NVEL, dtype=jnp.float32)
    factor = 0.5 * 4.0 ** (bin_ids / NVEL)
    shares = jnp.minimum(share_freq[:, None] * factor[None, :], 0.5)
    salt_share = jax.random.uniform(subkeys[1], (F, NVEL), minval=0.3, maxval=0.6)
    shares = jnp.where(bin_ids[None, :] >= NVEL - 16, salt_share, shares)
    raw_weights = jax.random.uniform(subkeys[2], (TAPS - 1, F, NVEL), minval=0.5, maxval=1.5)
    neighbour = jnp.sqrt(shares[None] * raw_weights / jnp.sum(raw_weights, axis=0, keepdims=True))
    weights = jnp.concatenate([jnp.sqrt(1.0 - shares)[None], neighbour], axis=0)
    base_phase = jax.random.uniform(subkeys[3], (1, F, NVEL), minval=-jnp.pi, maxval=jnp.pi)
    jitter = jax.random.uniform(subkeys[4], (TAPS, F, NVEL), minval=-0.5, maxval=0.5)
    jitter = jitter.at[0].set(0.0)
    phases = base_phase + jitter
    return jnp.stack([weights * jnp.cos(phases), weights * jnp.sin(phases)], axis=1).astype(jnp.float32)


def draw_velocity_bins(key, part):
    subkeys = jax.random.split(key, 4)
    chain_levels = SLABS * LEVELS
    sorted_positions = jax.random.permutation(subkeys[3], chain_levels)
    base_bins = jax.random.randint(subkeys[0], (chain_levels, 1, 1), 0, NVEL - 63)
    base_bins = jnp.where((sorted_positions == 2)[:, None, None], 0, base_bins)
    cell_velocity_groups = base_bins + jax.random.randint(subkeys[1], (chain_levels, CROSS, NXI), 0, 48)
    salt_velocity_groups = NVEL - 16 + jax.random.randint(subkeys[2], (chain_levels, CROSS, NXI), 0, 16)
    sudden_spike = (sorted_positions < 2)[:, None, None]
    selected_entry = jnp.where(sudden_spike, salt_velocity_groups, cell_velocity_groups)
    return selected_entry.reshape(SLABS, LEVELS, CROSS, NXI).astype(jnp.int32)


def draw_offset_list(key, part):
    subkeys = jax.random.split(key, 3)
    cross_shift = jax.random.randint(subkeys[0], (OFFS,), -OFF_Y, OFF_Y + 1)
    inline_shift = jax.random.randint(subkeys[1], (OFFS,), -OFF_X, OFF_X + 1)
    cross_shift = cross_shift.at[0].set(-OFF_Y).at[1].set(OFF_Y)
    inline_shift = inline_shift.at[2].set(-OFF_X).at[3].set(OFF_X)
    pairs = jnp.stack([cross_shift, inline_shift], axis=1)
    return pairs[jax.random.permutation(subkeys[2], OFFS)].astype(jnp.int32)


def steps_of(key, dims, cuts, smallest, largest):
    def one(position, shards_of):
        draws = jax.random.uniform(jax.random.fold_in(jax.random.fold_in(key, 6), position), (shards_of,), jnp.float32, smallest / len(cuts), largest / len(cuts))
        return jnp.repeat(jnp.exp(draws), dims[position] // shards_of).reshape((-1,) + (1,) * (len(dims) - position - 1))

    loudness = one(*cuts[0])
    for cut in cuts[1:]:
        loudness = loudness * one(*cut)
    return loudness


def gaussian(own_key, extent, width, reach, cuts=(), kind=jnp.bfloat16):
    result = jax.random.normal(own_key, extent, jnp.float32) * width
    if len(cuts) > 0:
        result = steps_of(own_key, extent, cuts, -0.22, 0.18) * result
    return jnp.clip(result, min=-reach, max=reach).astype(kind)


def setup_inputs(seed: int = 0) -> dict:
    splits = jax.random.split(jax.random.key(seed), 5)
    surface_fields = gaussian(splits[0], (2, 2, F, CROSS, NXI), 1.0, 6.0, ((3, 16),), jnp.float32)
    stencil_table = draw_stencil_table(jax.random.fold_in(splits[4], 71), 0)
    velocity_bins = draw_velocity_bins(jax.random.fold_in(splits[4], 71), 0)
    offset_list = draw_offset_list(jax.random.fold_in(splits[4], 71), 0)
    return {"surface_fields": surface_fields, "stencil_table": stencil_table, "velocity_bins": velocity_bins, "offset_list": offset_list}


tap_rows = (0, -4, -3, -2, -1, 1, 2, 3, 4, 0, 0, 0, 0)
tap_cols = (0, 0, 0, 0, 0, 0, 0, 0, 0, -2, -1, 1, 2)
reach_rows = 4
reach_cols = 2


def extrapolate(fields, coefficients):
    row_count = fields.shape[3] - 2 * reach_rows
    inline_width = fields.shape[4]
    padded = jnp.pad(fields, ((0, 0), (0, 0), (0, 0), (0, 0), (reach_cols, reach_cols)))
    conj_sign = jnp.array([1.0, -1.0], dtype=fields.dtype).reshape(2, 1, 1, 1)
    real_part = None
    imag_part = None
    for tap_index in range(len(tap_rows)):
        first_row = reach_rows + tap_rows[tap_index]
        first_col = reach_cols + tap_cols[tap_index]
        shifted = padded[:, :, :, first_row:first_row + row_count, first_col:first_col + inline_width]
        coef_real = coefficients[tap_index, 0]
        coef_imag = coefficients[tap_index, 1] * conj_sign
        term_real = coef_real * shifted[:, 0] - coef_imag * shifted[:, 1]
        term_imag = coef_real * shifted[:, 1] + coef_imag * shifted[:, 0]
        if tap_index == 0:
            real_part = term_real
            imag_part = term_imag
        else:
            real_part = real_part + term_real
            imag_part = imag_part + term_imag
    return jnp.stack([real_part, imag_part], axis=1)


def correlate(fields, offset_list):
    source = fields[0]
    receiver = fields[1]
    padded = jnp.pad(receiver, ((0, 0), (0, 0), (OFF_Y, OFF_Y), (OFF_X, OFF_X)))
    slice_shape = (2, source.shape[1], source.shape[2], source.shape[3])

    def one_offset(offset_couple):
        starts = (jnp.int32(0), jnp.int32(0), OFF_Y + offset_couple[0], OFF_X + offset_couple[1])
        shifted = lax.dynamic_slice(padded, starts, slice_shape)
        return jnp.sum(source[0] * shifted[0] + source[1] * shifted[1], axis=0)

    return lax.map(one_offset, offset_list)


def reference(surface_fields, stencil_table, velocity_bins, offset_list):
    def slab_step(fields, slab_velocity):
        for level_index in range(LEVELS):
            coefficients = jnp.take(stencil_table, slab_velocity[level_index], axis=3)
            padded = jnp.pad(fields, ((0, 0), (0, 0), (0, 0), (reach_rows, reach_rows), (0, 0)))
            fields = extrapolate(padded, coefficients)
        return fields, correlate(fields, offset_list)

    final_fields, images = lax.scan(slab_step, surface_fields, velocity_bins)
    return images
```

```python
import jax
import jax.numpy as jnp
from jax import lax
from jax.experimental import pallas as pl
from jax.experimental.pallas import tpu as pltpu
from jax.sharding import PartitionSpec as P

MESH = pl.DeviceIdType.MESH

OFF_Y = 8
TAPS = ((0, 0), (-4, 0), (-3, 0), (-2, 0), (-1, 0), (1, 0), (2, 0), (3, 0), (4, 0), (0, -2), (0, -1), (0, 1), (0, 2))
REACH = 4

LEVELS = 24
SLOTS = LEVELS // 2
ROWS = 32
BLOCKS = 8
HALF = 16
GRID = 256

UNITS = [ROWS // 8 + LEVELS - 1 - i for i in range(LEVELS)]
UNIT_BASE = [sum(UNITS[:i]) for i in range(LEVELS + 1)]
X_ROWS = [ROWS + 2 * REACH * (LEVELS - m) for m in range(LEVELS + 1)]
X_BASE = [sum(X_ROWS[:m]) for m in range(LEVELS + 1)]
BIN_PAD = REACH * LEVELS
BIN_ROWS = ROWS + 2 * BIN_PAD
GATHER = 6
CHUNK = 7


def stage_of(y):
    return jnp.minimum((y + 1) // 2, 3)


def stage_end(s):
    return jnp.where(s == 3, 32, 8 * s + 4)


def first_level(s):
    return jnp.where(s == 0, 16, jnp.where(s == 3, 0, 8))


def reach_blocks(s):
    return jnp.where(s == 3, 3, 2)


def worker(s, p, b):
    return 4 * (jnp.maximum(2 * s - 1, 0) + p // 2) + p % 2, 2 * b + jnp.where(s == 0, 1, 0)


def halo_blocks(q):
    return (REACH * (LEVELS - 1 - 2 * q) + HALF - 1) // HALF


def both(*conditions):
    out = conditions[0]
    for c in conditions[1:]:
        out = jnp.logical_and(out, c)
    return out


def chain_kernel(
    surf_ref, tab_ref, bins_ref, out_s, out_r,
    x_all, coef, bins_all, tab8, surf, im_s, im_r,
    bin_send, bin_recv, surf_send, surf_recv, hop_send, hop_recv, im_send, ims_recv, imr_recv, hello,
):
    d, j = lax.axis_index("depth"), lax.axis_index("xline")
    y, zh, bj, core = d // 4, d % 4, j // 2, j % 2
    so = stage_of(y)
    qo = d - stage_end(so) + SLOTS
    ho = halo_blocks(qo)
    sw = jnp.where(core == 1, 0, (y + 1) // 2)
    yw = y - jnp.maximum(2 * sw - 1, 0)
    is_w = both(zh <= 1, jnp.where(core == 1, y <= 1, both(y >= 1, y <= 6)))
    p, b = 2 * yw + zh, bj
    i0 = first_level(sw)
    q0 = i0 // 2
    ew = stage_end(sw)
    is_surf = both(y <= 1, zh <= 1)

    def me(target):
        return both(target[0] == d, target[1] == j)

    def other(target):
        return jnp.logical_not(me(target))

    def inside(block):
        return both(block >= 0, block < BLOCKS)

    def row_inside(jj):
        return both(jj >= 0, jj < 2 * BLOCKS)

    def bin_targets():
        for pp in range(4):
            for db in (0, -1, 1, -2, 2, -3, 3):
                bb = bj + db
                near = both(j >= 2 * bb - ho, j <= 2 * bb + 1 + ho)
                yield pp, db, bb, both(inside(bb), near), worker(so, pp, bb)

    def surf_targets():
        for db in (0, -1, 1):
            bb = bj + db
            yield db, bb, both(is_surf, inside(bb)), (d, 2 * bb + 1)

    def stage_targets(s, on):
        for db in (0, -1, 1, -2, 2, -3, 3):
            bb = b + db
            yield db, bb, both(on, inside(bb), abs(db) <= reach_blocks(jnp.maximum(s, sw))), worker(s, p, bb)

    is_later = both(is_w, sw >= 1)
    is_earlier = both(is_w, sw <= 2)

    barrier = pltpu.get_barrier_semaphore()

    def greet(target):
        pl.semaphore_signal(barrier, inc=1, device_id=target, device_id_type=MESH)

    @pl.when(is_w)
    def _():
        for g in range(6):
            source = (d, 2 * b - 2 + g)

            @pl.when(both(sw == 0, row_inside(source[1]), other(source)))
            def _():
                greet(source)

        def slot(q, c):
            h = halo_blocks(q)
            for g in range(2 * BIN_PAD // HALF + 2):
                source = (ew - SLOTS + q, 2 * b - 6 + g)

                @pl.when(both(row_inside(source[1]), g - 6 >= -h, g - 6 <= 1 + h, other(source)))
                def _():
                    greet(source)

            return c

        lax.fori_loop(q0, SLOTS, slot, 0)
        for db, bb, on, target in stage_targets(sw + 1, is_earlier):

            @pl.when(on)
            def _():
                greet(target)

    for part in range(2):
        block = surf_ref[jnp.minimum(y, 1), part, jnp.minimum(zh, 1)]
        surf[part] = block if part == 0 else jnp.where(y == 1, -block, block)
    zeros8 = jnp.zeros((2, OFF_Y, 128), jnp.float32)
    for f in range(2):

        @pl.when(j == 0)
        def _():
            im_r[f, :, 0:8, :] = zeros8

        @pl.when(j == 2 * BLOCKS - 1)
        def _():
            im_r[f, :, 24:32, :] = zeros8

    def x_row(level):
        base = level * (ROWS + 2 * REACH * LEVELS) - REACH * level * (level - 1)
        return pl.multiple_of(base, 8), pl.multiple_of(REACH * (LEVELS - level), 8)

    @pl.when(is_w)
    def _():
        f = p % 2
        for t in range(2 * len(TAPS)):
            tab8[t] = jnp.broadcast_to(tab_ref[t // 2, t % 2, pl.ds(f, 1), :], (8, 128))
        base, own = x_row(i0)
        zf = jnp.zeros((2, HALF, 128), jnp.float32)
        zi = jnp.zeros((2, HALF, 128), jnp.int32)
        for g in range(2 * BIN_PAD // HALF + 2):
            jj = 2 * b - 6 + g

            @pl.when(jnp.logical_not(row_inside(jj)))
            def _():
                def clear(q, c):
                    bins_all[q, :, pl.ds(HALF * g, HALF), :] = zi
                    return c

                lax.fori_loop(q0, SLOTS, clear, 0)
                row = own + HALF * (g - 6)

                @pl.when(both(row >= 0, HALF * (g - 6) < ROWS + own))
                def _():
                    x_all[:, pl.ds(pl.multiple_of(base + row, 8), HALF), :] = zf

    waits = jnp.int32(0)
    for pp, db, bb, on, target in bin_targets():
        waits += jnp.where(both(on, other(target)), 1, 0)
    for db, bb, on, target in surf_targets():
        waits += jnp.where(both(on, other(target)), 1, 0)
    for db, bb, on, target in stage_targets(sw - 1, is_later):
        waits += jnp.where(on, 1, 0)
    pl.semaphore_wait(barrier, waits)

    def surf_copy(db, bb, target):
        row = X_BASE[16] + 32 + HALF * (j - 2 * bb)
        return pltpu.make_async_remote_copy(
            src_ref=surf, dst_ref=x_all.at[:, pl.ds(pl.multiple_of(row, 8), HALF), :],
            send_sem=surf_send.at[db + 1], recv_sem=surf_recv.at[j - 2 * bb + 2],
            device_id=target, device_id_type=MESH)

    for db, bb, on, target in surf_targets():

        @pl.when(both(on, other(target)))
        def _():
            surf_copy(db, bb, target).start()

        @pl.when(both(on, me(target)))
        def _():
            row = X_BASE[16] + 32 + HALF * (j - 2 * bb)
            x_all[:, pl.ds(pl.multiple_of(row, 8), HALF), :] = surf[...]

    def bin_copy(pp, db, bb, target):
        g = j - 2 * bb + 6
        return pltpu.make_async_remote_copy(
            src_ref=bins_ref.at[0], dst_ref=bins_all.at[qo, :, pl.ds(pl.multiple_of(HALF * g, HALF), HALF), :],
            send_sem=bin_send.at[pp, db + 3], recv_sem=bin_recv.at[qo, g],
            device_id=target, device_id_type=MESH)

    for pp, db, bb, on, target in bin_targets():

        @pl.when(both(on, other(target)))
        def _():
            bin_copy(pp, db, bb, target).start()

        @pl.when(both(on, me(target)))
        def _():
            g = j - 2 * bb + 6
            bins_all[qo, :, pl.ds(pl.multiple_of(HALF * g, HALF), HALF), :] = bins_ref[0]

    for db, bb, on, target in stage_targets(sw - 1, is_later):

        @pl.when(on)
        def _():
            pl.semaphore_signal(hello, inc=1, device_id=target, device_id_type=MESH)

    def hop_copy(db, bb, target):
        base, own = x_row(first_level(sw + 1))
        row = base + own - ROWS * db
        return pltpu.make_async_remote_copy(
            src_ref=x_all.at[:, pl.ds(X_BASE[LEVELS], ROWS), :],
            dst_ref=x_all.at[:, pl.ds(pl.multiple_of(row, 8), ROWS), :],
            send_sem=hop_send.at[db + 3], recv_sem=hop_recv.at[3 - db],
            device_id=target, device_id_type=MESH)

    def image_copy(src, dst, q, k, recv, target):
        return pltpu.make_async_remote_copy(
            src_ref=src, dst_ref=dst, send_sem=im_send.at[q, k], recv_sem=recv,
            device_id=target, device_id_type=MESH)

    def image_targets(q):
        row = X_BASE[2 * q + 2] + REACH * (LEVELS - 2 * q - 2)
        dd = ew - SLOTS + q
        yield 0, 0, p < 2, (dd, 2 * b), row, 16, 0, 0
        yield 0, 1, p < 2, (dd, 2 * b + 1), row + 16, 16, 0, 0
        yield 1, 0, p >= 2, (dd, 2 * b), row, 24, 8, 0
        yield 1, 1, p >= 2, (dd, 2 * b + 1), row + 8, 24, 0, 0
        yield 1, 2, both(p >= 2, b > 0), (dd, 2 * b - 1), row, 8, 24, 1
        yield 1, 3, both(p >= 2, b < BLOCKS - 1), (dd, 2 * b + 2), row + 24, 8, 0, 1

    def image_refs(r, row, rows, to, which):
        f = p % 2
        src = x_all.at[:, pl.ds(row, rows), :]
        if r == 0:
            return src, im_s.at[f], ims_recv.at[f]
        return src, im_r.at[f, :, pl.ds(to, rows), :], imr_recv.at[f, which]

    def apply(i):
        n, base, out = UNITS[i], X_BASE[i], X_BASE[i + 1]
        pieces = -(-n // CHUNK)
        cuts = [n * k // pieces for k in range(pieces + 1)]
        for u0, u1 in zip(cuts, cuts[1:]):
            r, rows = 8 * u0, 8 * (u1 - u0)
            unit = 8 * (UNIT_BASE[i] + u0)
            rr = ii = ri = ir = None
            for t, (dy, dx) in enumerate(TAPS):
                cr, ci = coef[2 * t, unit : unit + rows, :], coef[2 * t + 1, unit : unit + rows, :]
                at = base + r + REACH + dy
                fr, fi = x_all[0, at : at + rows, :], x_all[1, at : at + rows, :]
                if dx != 0:
                    fr, fi = pltpu.roll(fr, (-dx) % 128, 1), pltpu.roll(fi, (-dx) % 128, 1)
                if rr is None:
                    rr, ii, ri, ir = cr * fr, ci * fi, cr * fi, ci * fr
                else:
                    rr, ii, ri, ir = rr + cr * fr, ii + ci * fi, ri + cr * fi, ir + ci * fr
            x_all[0, out + r : out + r + rows, :] = rr - ii
            x_all[1, out + r : out + r + rows, :] = ri + ir

    @pl.when(is_w)
    def _():
        lane = lax.broadcasted_iota(jnp.int32, (8, 128), 1)
        sub = lax.broadcasted_iota(jnp.int32, (8, 128), 0)

        def slot(q, c):
            h = halo_blocks(q)
            for g in range(2 * BIN_PAD // HALF + 2):
                source = (ew - SLOTS + q, 2 * b - 6 + g)

                @pl.when(both(row_inside(source[1]), g - 6 >= -h, g - 6 <= 1 + h, other(source)))
                def _():
                    pltpu.make_async_remote_copy(
                        src_ref=bins_ref.at[0], dst_ref=bins_all.at[q, :, pl.ds(HALF * g, HALF), :],
                        send_sem=bin_send.at[0, 0], recv_sem=bin_recv.at[q, g],
                        device_id=source, device_id_type=MESH).wait_recv()

            for step in range(2):
                i = 2 * q + step
                n = ROWS // 8 + LEVELS - 1 - i
                first = (ROWS // 8 + LEVELS - 1) * i - i * (i - 1) // 2

                def group(k, cc):
                    u = jnp.maximum(jnp.minimum(k * GATHER, n - GATHER), 0)
                    for e in range(GATHER):
                        row = REACH + REACH * i + 8 * (u + e)
                        index = bins_all[q, step, pl.ds(row, 8), :]
                        line = ROWS * b - REACH * (LEVELS - 1 - i) + 8 * (u + e) + sub
                        valid = both(line >= 0, line < GRID)
                        to = pl.multiple_of(8 * (first + u + e), 8)
                        for t, (dy, dx) in enumerate(TAPS):
                            keep = valid
                            if dx > 0:
                                keep = both(valid, lane < 128 - dx)
                            elif dx < 0:
                                keep = both(valid, lane >= -dx)
                            for part in range(2):
                                value = jnp.take_along_axis(
                                    tab8[2 * t + part], index, axis=1, mode="promise_in_bounds")
                                coef[2 * t + part, pl.ds(to, 8), :] = jnp.where(keep, value, 0.0)
                    return cc

                lax.fori_loop(0, (n + GATHER - 1) // GATHER, group, 0)
            return c

        lax.fori_loop(q0, SLOTS, slot, 0)

        for g in range(6):
            source = (d, 2 * b - 2 + g)

            @pl.when(both(sw == 0, row_inside(source[1]), other(source)))
            def _():
                pltpu.make_async_remote_copy(
                    src_ref=surf, dst_ref=x_all.at[:, pl.ds(X_BASE[16] + HALF * g, HALF), :],
                    send_sem=surf_send.at[0], recv_sem=surf_recv.at[g],
                    device_id=source, device_id_type=MESH).wait_recv()

        base, own = x_row(i0)
        for db, bb, on, target in stage_targets(sw - 1, is_later):

            @pl.when(on)
            def _():
                row = base + own + ROWS * db
                pltpu.make_async_remote_copy(
                    src_ref=x_all.at[:, pl.ds(X_BASE[LEVELS], ROWS), :],
                    dst_ref=x_all.at[:, pl.ds(pl.multiple_of(row, 8), ROWS), :],
                    send_sem=hop_send.at[0], recv_sem=hop_recv.at[db + 3],
                    device_id=target, device_id_type=MESH).wait_recv()

        for q in range(SLOTS):

            @pl.when(q >= q0)
            def _():
                apply(2 * q)
                apply(2 * q + 1)
                if q == SLOTS - 1:
                    count = jnp.int32(0)
                    for db, bb, on, target in stage_targets(sw + 1, is_earlier):
                        count += jnp.where(on, 1, 0)

                    @pl.when(is_earlier)
                    def _():
                        pl.semaphore_wait(hello, count)

                    for db, bb, on, target in stage_targets(sw + 1, is_earlier):

                        @pl.when(on)
                        def _():
                            hop_copy(db, bb, target).start()

                for r, k, on, target, row, rows, to, which in image_targets(q):
                    src, dst, recv = image_refs(r, row, rows, to, which)

                    @pl.when(both(on, other(target)))
                    def _():
                        image_copy(src, dst, q, k, recv, target).start()

                    @pl.when(both(on, me(target)))
                    def _():
                        dst[...] = src[...]

    def sources(f):
        yield both(True, other(worker(so, f, bj))), im_s.at[f], ims_recv.at[f]
        for odd in range(2):
            mine = core == odd
            yield both(mine, other(worker(so, 2 + f, bj))), im_r.at[f, :, pl.ds(8 - 8 * odd, 24), :], imr_recv.at[f, 0]
            beside = bj + 2 * odd - 1
            yield (both(mine, inside(beside), other(worker(so, 2 + f, beside))),
                   im_r.at[f, :, pl.ds(24 * odd, 8), :], imr_recv.at[f, 1])

    for f in range(2):
        for on, dst, recv in sources(f):

            @pl.when(on)
            def _():
                pltpu.make_async_remote_copy(
                    src_ref=dst, dst_ref=dst, send_sem=im_send.at[0, 0], recv_sem=recv,
                    device_id=(d, j ^ 1), device_id_type=MESH).wait_recv()

    out_s[...] = im_s[...]
    out_r[...] = im_r[...]

    for db, bb, on, target in surf_targets():

        @pl.when(both(on, other(target)))
        def _():
            surf_copy(db, bb, target).wait_send()

    for pp, db, bb, on, target in bin_targets():

        @pl.when(both(on, other(target)))
        def _():
            bin_copy(pp, db, bb, target).wait_send()

    @pl.when(is_w)
    def _():
        for db, bb, on, target in stage_targets(sw + 1, is_earlier):

            @pl.when(on)
            def _():
                hop_copy(db, bb, target).wait_send()

        for q in range(SLOTS):
            for r, k, on, target, row, rows, to, which in image_targets(q):
                src, dst, recv = image_refs(r, row, rows, to, which)

                @pl.when(both(q >= q0, on, other(target)))
                def _():
                    image_copy(src, dst, q, k, recv, target).wait_send()


def image_kernel(offsets, s_ref, r_ref, out_ref):
    lane = lax.broadcasted_iota(jnp.int32, (HALF, 128), 1)
    for h in range(out_ref.shape[1]):
        hy, hx = offsets[h, 0], offsets[h, 1]
        total = None
        for f in range(2):
            for part in range(2):
                moved = r_ref[f, part, pl.ds(OFF_Y + hy, HALF), :]
                moved = pltpu.roll(moved, lax.rem(128 - hx, 128), 1)
                term = s_ref[f, part] * moved
                total = term if total is None else total + term if part == 0 else total - term
        valid = both(lane + hx >= 0, lane + hx < 128)
        out_ref[0, h] = jnp.where(valid, total, 0.0)


def shards(surface_fields, stencil_table, velocity_bins, offset_list):
    vmem = pl.BlockSpec(memory_space=pltpu.VMEM)
    f32 = jnp.float32
    dma = pltpu.SemaphoreType.DMA
    source, receiver = pl.pallas_call(
        chain_kernel,
        out_shape=(jax.ShapeDtypeStruct((2, 2, 16, 128), f32), jax.ShapeDtypeStruct((2, 2, 32, 128), f32)),
        in_specs=[vmem] * 3,
        out_specs=(vmem, vmem),
        scratch_shapes=[
            pltpu.VMEM((2, sum(X_ROWS), 128), f32),
            pltpu.VMEM((2 * len(TAPS), 8 * (UNIT_BASE[LEVELS] + GATHER), 128), f32),
            pltpu.VMEM((SLOTS, 2, BIN_ROWS, 128), jnp.int32),
            pltpu.VMEM((2 * len(TAPS), 8, 128), f32),
            pltpu.VMEM((2, HALF, 128), f32),
            pltpu.VMEM((2, 2, 16, 128), f32),
            pltpu.VMEM((2, 2, 32, 128), f32),
            dma((4, 7)), dma((SLOTS, 14)), dma((3,)), dma((6,)), dma((7,)), dma((7,)),
            dma((SLOTS, 4)), dma((2,)), dma((2, 2)), pltpu.SemaphoreType.REGULAR,
        ],
        compiler_params=pltpu.CompilerParams(
            collective_id=0, has_side_effects=True, vmem_limit_bytes=56 * 2**20),
    )(surface_fields, stencil_table, velocity_bins)
    return pl.pallas_call(
        image_kernel,
        out_shape=jax.ShapeDtypeStruct((1, offset_list.shape[0], HALF, 128), f32),
        in_specs=[pl.BlockSpec(memory_space=pltpu.SMEM), vmem, vmem],
        out_specs=vmem,
    )(offset_list, source, receiver)


def solution(mesh):
    return jax.shard_map(
        shards,
        mesh=mesh,
        in_specs=(P(None, None, None, "xline", None), P(), P("depth", None, "xline", None), P()),
        out_specs=P("depth", None, "xline", None),
        check_vma=False,
    )
```

```python
import jax
import jax.numpy as jnp
from jax import lax
from jax.experimental import pallas as pl
from jax.experimental.pallas import tpu as pltpu
from jax.sharding import PartitionSpec as P

MESH = pl.DeviceIdType.MESH

OFF_Y = 8
TAPS = ((0, 0), (-4, 0), (-3, 0), (-2, 0), (-1, 0), (1, 0), (2, 0), (3, 0), (4, 0), (0, -2), (0, -1), (0, 1), (0, 2))
REACH = 4

LEVELS = 24
SLOTS = LEVELS // 2
ROWS = 32
BLOCKS = 8
HALF = 16
GRID = 256

UNITS = [ROWS // 8 + LEVELS - 1 - i for i in range(LEVELS)]
UNIT_BASE = [sum(UNITS[:i]) for i in range(LEVELS + 1)]
X_ROWS = [ROWS + 2 * REACH * (LEVELS - m) for m in range(LEVELS + 1)]
X_BASE = [sum(X_ROWS[:m]) for m in range(LEVELS + 1)]
BIN_PAD = REACH * LEVELS
BIN_ROWS = ROWS + 2 * BIN_PAD
GATHER = 6
CHUNK = 7


def stage_of(y):
    return jnp.minimum((y + 1) // 2, 3)


def stage_end(s):
    return jnp.where(s == 3, 32, 8 * s + 4)


def first_level(s):
    return jnp.where(s == 0, 16, jnp.where(s == 3, 0, 8))


def reach_blocks(s):
    return jnp.where(s == 3, 3, 2)


def worker(s, p, b):
    return 4 * (jnp.maximum(2 * s - 1, 0) + p // 2) + p % 2, 2 * b + jnp.where(s == 0, 1, 0)


def halo(level):
    return REACH * (LEVELS - 1 - level)


def sent_halo(q):
    return -(-halo(2 * q) // 8) * 8


def both(*conditions):
    out = conditions[0]
    for c in conditions[1:]:
        out = jnp.logical_and(out, c)
    return out


def chain_kernel(
    surf_ref, tab_hbm, bins_ref, out_s, out_r,
    x_all, coef, bins_all, tab8, tab_ref, zero_rows,
    tab_sem, self_sem, zero_sem, bin_send, bin_recv, edge_send, fwd_send, fwd_recv, surf_send, surf_recv, hop_send, hop_recv,
    im_send, ims_recv, imr_recv, hello,
):
    d, j = lax.axis_index("depth"), lax.axis_index("xline")
    y, zh, bj, core = d // 4, d % 4, j // 2, j % 2
    so = stage_of(y)
    qo = d - stage_end(so) + SLOTS
    sw = jnp.where(core == 1, 0, (y + 1) // 2)
    yw = y - jnp.maximum(2 * sw - 1, 0)
    is_w = both(zh <= 1, jnp.where(core == 1, y <= 1, both(y >= 1, y <= 6)))
    p, b = 2 * yw + zh, bj
    i0 = first_level(sw)
    q0 = i0 // 2
    ew = stage_end(sw)
    is_surf = both(y <= 1, zh <= 1)
    self_slot = both(so == sw, is_w)

    def me(target):
        return both(target[0] == d, target[1] == j)

    def other(target):
        return jnp.logical_not(me(target))

    def inside(block):
        return both(block >= 0, block < BLOCKS)

    def remote(src, dst, send, recv, target):
        return pltpu.make_async_remote_copy(
            src_ref=src, dst_ref=dst, send_sem=send, recv_sem=recv, device_id=target, device_id_type=MESH)

    def surf_targets():
        for db in (0, -1, 1):
            bb = bj + db
            yield db, both(is_surf, inside(bb)), (d, 2 * bb + 1)

    def stage_targets(s, on):
        for db in (0, -1, 1, -2, 2, -3, 3):
            bb = b + db
            near = True if abs(db) <= 2 else reach_blocks(jnp.maximum(s, sw)) == 3
            yield db, both(on, inside(bb), near), worker(s, p, bb)

    SIDES = (-1, 1, -2, 2, -3, 3)

    def beside():
        for e, db in enumerate(SIDES):
            far = 1 if abs(db) == 1 else jnp.where(sw == 0, 0, jnp.where(sw == 3, 1, 1 if abs(db) == 2 else 0))
            yield e, db, both(is_w, inside(b + db), far == 1), worker(sw, p, b + db)

    is_later = both(is_w, sw >= 1)
    is_earlier = both(is_w, sw <= 2)
    edge_block = bj + 2 * core - 1
    edge_on = both(qo == SLOTS - 1, inside(edge_block))

    barrier = pltpu.get_barrier_semaphore()

    def greet(target):
        pl.semaphore_signal(barrier, inc=1, device_id=target, device_id_type=MESH)

    tab_copy = pltpu.make_async_copy(tab_hbm, tab_ref, tab_sem)

    @pl.when(is_w)
    def _():
        tab_copy.start()

        @pl.when(sw == 0)
        def _():
            for g in range(6):
                source = (d, 2 * b - 2 + g)

                @pl.when(both(source[1] >= 0, source[1] < 2 * BLOCKS, g != 3))
                def _():
                    greet(source)

        def slot(q, c):
            mine = both(self_slot, q == qo)

            @pl.when(jnp.logical_not(both(mine, core == 0)))
            def _():
                greet((ew - SLOTS + q, 2 * b))

            @pl.when(jnp.logical_not(both(mine, core == 1)))
            def _():
                greet((ew - SLOTS + q, 2 * b + 1))

            return c

        lax.fori_loop(q0, SLOTS, slot, 0)
        for db, on, target in stage_targets(sw + 1, is_earlier):

            @pl.when(on)
            def _():
                greet(target)

        for e, db, on, target in beside():

            @pl.when(on)
            def _():
                greet(target)

        @pl.when(b > 0)
        def _():
            greet((ew - 1, 2 * b - 1))

        @pl.when(b < BLOCKS - 1)
        def _():
            greet((ew - 1, 2 * b + 2))

    zero_rows[...] = jnp.zeros((2, 2, OFF_Y, 128), jnp.float32)

    def zero_copy():
        return pltpu.make_async_copy(
            zero_rows, out_r.at[:, :, pl.ds(pl.multiple_of(24 * core, 8), OFF_Y), :], zero_sem)

    at_edge = jnp.logical_not(inside(edge_block))

    @pl.when(at_edge)
    def _():
        zero_copy().start()

    def x_row(level):
        base = level * (ROWS + 2 * REACH * LEVELS) - REACH * level * (level - 1)
        return pl.multiple_of(base, 8), pl.multiple_of(REACH * (LEVELS - level), 8)

    count = jnp.int32(0)
    for pp in range(4):
        count += jnp.where(other(worker(so, pp, bj)), 1, 0)
    count += jnp.where(edge_on, 4, 0)
    for db, on, target in surf_targets():
        count += jnp.where(both(on, other(target)), 1, 0)
    for db, on, target in stage_targets(sw - 1, is_later):
        count += jnp.where(on, 1, 0)
    for e, db, on, target in beside():
        count += jnp.where(on, 1, 0)
    pl.semaphore_wait(barrier, count)

    own_rows = pl.multiple_of(BIN_PAD + HALF * core, HALF)

    def bin_copy(pp):
        return remote(bins_ref.at[0], bins_all.at[qo, :, pl.ds(own_rows, HALF), :],
                      bin_send.at[pp], bin_recv.at[qo], worker(so, pp, bj))

    def edge_copy(pp):
        start = pl.multiple_of(8 * core, 8)
        to = pl.multiple_of(jnp.where(core == 1, BIN_PAD - 8, BIN_PAD + ROWS), 8)
        return remote(bins_ref.at[0, :, pl.ds(start, 8), :], bins_all.at[SLOTS - 1, :, pl.ds(to, 8), :],
                      edge_send.at[pp], fwd_recv.at[SLOTS - 1, 1 - core], worker(so, pp, edge_block))

    surf_block = surf_ref.at[jnp.minimum(y, 1), :, jnp.minimum(zh, 1)]

    def surf_row():
        return X_BASE[16] + 32 + HALF * core

    def surf_copy(db, target):
        row = pl.multiple_of(surf_row() - ROWS * db, 8)
        return remote(surf_block, x_all.at[:, pl.ds(row, HALF), :], surf_send.at[db + 1],
                      surf_recv.at[core - 2 * db + 2], target)

    def self_bins():
        return pltpu.make_async_copy(
            bins_ref.at[0], bins_all.at[qo, :, pl.ds(own_rows, HALF), :], self_sem.at[0])

    def self_surf():
        return pltpu.make_async_copy(
            surf_block, x_all.at[:, pl.ds(X_BASE[16] + 32 + HALF, HALF), :], self_sem.at[1])

    for pp in range(4):
        target = worker(so, pp, bj)

        @pl.when(other(target))
        def _():
            bin_copy(pp).start()

        @pl.when(me(target))
        def _():
            self_bins().start()

    @pl.when(edge_on)
    def _():
        for pp in range(4):
            edge_copy(pp).start()

    @pl.when(is_surf)
    def _():
        for db, on, target in surf_targets():

            @pl.when(both(on, other(target)))
            def _():
                surf_copy(db, target).start()

            @pl.when(both(on, me(target)))
            def _():
                self_surf().start()

    @pl.when(is_later)
    def _():
        for db, on, target in stage_targets(sw - 1, is_later):

            @pl.when(on)
            def _():
                pl.semaphore_signal(hello, inc=1, device_id=target, device_id_type=MESH)

    def forwards(q):
        for e, db, on, target in beside():
            rows = min(ROWS, sent_halo(q) - ROWS * (abs(db) - 1))
            if rows > 0:
                start = BIN_PAD if db < 0 else BIN_PAD + ROWS - rows
                src = bins_all.at[q, :, start : start + rows, :]
                to = start - ROWS * db
                dst = bins_all.at[q, :, to : to + rows, :]
                send = fwd_send.at[6 * (q % 4) + e if q < 8 else 24 + 2 * (q - 8) + e]
                yield on, remote(src, dst, send, fwd_recv.at[q, 0 if db > 0 else 1], target)

    def wait_sent(*slots):
        for q in slots:
            for on, copy in forwards(q):

                @pl.when(on)
                def _():
                    copy.wait_send()

    def wait_own(q):
        here = both(self_slot, q == qo)

        @pl.when(jnp.logical_not(here))
        def _():
            dst = bins_all.at[q, :, BIN_PAD : BIN_PAD + ROWS, :]
            remote(dst, dst, bin_send.at[0], bin_recv.at[q], (ew - SLOTS + q, 2 * b)).wait_recv()

        @pl.when(here)
        def _():
            dst = bins_all.at[q, :, pl.ds(pl.multiple_of(BIN_PAD + HALF * (1 - core), HALF), HALF), :]
            remote(dst, dst, bin_send.at[0], bin_recv.at[q], (d, j + 1 - 2 * core)).wait_recv()
            self_bins().wait()

    def forward(*slots):
        for q in slots:
            wait_own(q)
            for on, copy in forwards(q):

                @pl.when(on)
                def _():
                    copy.start()

    def wait_forwarded(*slots):
        for q in slots:
            rows_all = sent_halo(q)
            deepest = -(-rows_all // ROWS)
            for side in range(2):
                there = b if side == 0 else BLOCKS - 1 - b
                for k in range(1, deepest + 1):
                    rows = min(rows_all, ROWS * k)
                    start = BIN_PAD - rows if side == 0 else BIN_PAD + ROWS
                    dst = bins_all.at[q, :, start : start + rows, :]

                    @pl.when(there >= k if k == deepest else there == k)
                    def _():
                        remote(dst, dst, bin_send.at[0], fwd_recv.at[q, side], (d, j + 1 - 2 * core)).wait_recv()

    def hop_copy(db, target):
        base, own = x_row(first_level(sw + 1))
        row = pl.multiple_of(base + own - ROWS * db, 8)
        return remote(x_all.at[:, pl.ds(X_BASE[LEVELS], ROWS), :], x_all.at[:, pl.ds(row, ROWS), :],
                      hop_send.at[db + 3], hop_recv.at[3 - db], target)

    def source_images(q, row):
        dd, f = ew - SLOTS + q, p % 2
        for half in range(2):
            yield half, remote(x_all.at[:, pl.ds(pl.multiple_of(row + HALF * half, 8), HALF), :], out_s.at[f],
                               im_send.at[q % 4, half], ims_recv.at[f], (dd, 2 * b + half))

    def receiver_images(q, row):
        dd, f = ew - SLOTS + q, p % 2
        for half in range(2):
            yield half, remote(x_all.at[:, pl.ds(pl.multiple_of(row + 8 * half, 8), 24), :],
                               out_r.at[f, :, pl.ds(8 - 8 * half, 24), :],
                               im_send.at[q % 4, half], imr_recv.at[f, 0], (dd, 2 * b + half))

    def edge_images(q, row):
        dd, f = ew - SLOTS + q, p % 2
        for half in range(2):
            on = b > 0 if half == 0 else b < BLOCKS - 1
            yield on, remote(x_all.at[:, pl.ds(pl.multiple_of(row + 24 * half, 8), 8), :],
                             out_r.at[f, :, pl.ds(24 - 24 * half, 8), :],
                             im_send.at[q % 4, 2 + half], imr_recv.at[f, 1], (dd, 2 * b - 1 + 3 * half))

    def send_images(q, level):
        base, own = x_row(level) if not isinstance(level, int) else (X_BASE[level], REACH * (LEVELS - level))
        row = base + own
        mine = both(self_slot, q == qo)

        def pair(images, local):
            for half, copy in images(q, row):
                here = both(mine, core == half)

                @pl.when(jnp.logical_not(here))
                def _():
                    copy.start()

                @pl.when(here)
                def _():
                    local(half)

        def local_source(half):
            copy = pltpu.make_async_copy(
                x_all.at[:, pl.ds(pl.multiple_of(row + HALF * half, 8), HALF), :], out_s.at[p % 2], self_sem.at[2])
            copy.start()
            copy.wait()

        def local_receiver(half):
            copy = pltpu.make_async_copy(
                x_all.at[:, pl.ds(pl.multiple_of(row + 8 * half, 8), 24), :],
                out_r.at[p % 2, :, pl.ds(8 - 8 * half, 24), :], self_sem.at[2])
            copy.start()
            copy.wait()

        @pl.when(p < 2)
        def _():
            pair(source_images, local_source)

        @pl.when(p >= 2)
        def _():
            pair(receiver_images, local_receiver)
            for on, copy in edge_images(q, row):

                @pl.when(on)
                def _():
                    copy.start()

    def wait_images(q):
        base, own = x_row(2 * q + 2)
        mine = both(self_slot, q == qo)

        def pair(images):
            for half, copy in images(q, base + own):

                @pl.when(jnp.logical_not(both(mine, core == half)))
                def _():
                    copy.wait_send()

        @pl.when(p < 2)
        def _():
            pair(source_images)

        @pl.when(p >= 2)
        def _():
            pair(receiver_images)
            for on, copy in edge_images(q, base + own):

                @pl.when(on)
                def _():
                    copy.wait_send()

    def apply(i):
        n, base, out = UNITS[i], X_BASE[i], X_BASE[i + 1]
        pieces = -(-n // CHUNK)
        cuts = [n * k // pieces for k in range(pieces + 1)]
        for u0, u1 in zip(cuts, cuts[1:]):
            r, rows = 8 * u0, 8 * (u1 - u0)
            unit = 8 * (UNIT_BASE[i] + u0)
            rr = ii = ri = ir = None
            for t, (dy, dx) in enumerate(TAPS):
                cr, ci = coef[2 * t, unit : unit + rows, :], coef[2 * t + 1, unit : unit + rows, :]
                at = base + r + REACH + dy
                fr, fi = x_all[0, at : at + rows, :], x_all[1, at : at + rows, :]
                if dx != 0:
                    fr, fi = pltpu.roll(fr, (-dx) % 128, 1), pltpu.roll(fi, (-dx) % 128, 1)
                if rr is None:
                    rr, ii, ri, ir = cr * fr, ci * fi, cr * fi, ci * fr
                else:
                    rr, ii, ri, ir = rr + cr * fr, ii + ci * fi, ri + cr * fi, ir + ci * fr
            x_all[0, out + r : out + r + rows, :] = rr - ii
            x_all[1, out + r : out + r + rows, :] = ri + ir

    def look_up(q, size):
        lane = lax.broadcasted_iota(jnp.int32, (8, 128), 1)
        sub = lax.broadcasted_iota(jnp.int32, (8, 128), 0)
        for step in range(2):
            i = 2 * q + step
            n = ROWS // 8 + LEVELS - 1 - i
            first = (ROWS // 8 + LEVELS - 1) * i - i * (i - 1) // 2

            def group(k, c):
                u = jnp.minimum(k * size, n - size)
                for e in range(size):
                    row = REACH + REACH * i + 8 * (u + e)
                    index = bins_all[q, step, pl.ds(row, 8), :]
                    line = ROWS * b - REACH * (LEVELS - 1 - i) + 8 * (u + e) + sub
                    valid = both(line >= 0, line < GRID)
                    to = pl.multiple_of(8 * (first + u + e), 8)
                    for t, (dy, dx) in enumerate(TAPS):
                        keep = valid
                        if dx > 0:
                            keep = both(valid, lane < 128 - dx)
                        elif dx < 0:
                            keep = both(valid, lane >= -dx)
                        for part in range(2):
                            value = jnp.take_along_axis(
                                tab8[2 * t + part], index, axis=1, mode="promise_in_bounds")
                            coef[2 * t + part, pl.ds(to, 8), :] = jnp.where(keep, value, 0.0)
                return c

            lax.fori_loop(0, (n + size - 1) // size, group, 0)

    def look_up_slots(start, end):
        def slot(q, c):
            look_up(q, GATHER)
            return c

        lax.fori_loop(start, end, slot, 0)

    @pl.when(is_w)
    def _():
        f = p % 2
        tab_copy.wait()
        for t in range(2 * len(TAPS)):
            tab8[t] = jnp.broadcast_to(tab_ref[t // 2, t % 2, pl.ds(f, 1), :], (8, 128))
        base, own = x_row(i0)
        zf = jnp.zeros((2, ROWS, 128), jnp.float32)
        zi = jnp.zeros((2, ROWS, 128), jnp.int32)
        for db in SIDES:

            @pl.when(jnp.logical_not(inside(b + db)))
            def _():
                def clear(q, c):
                    bins_all[q, :, pl.ds(BIN_PAD + ROWS * db, ROWS), :] = zi
                    return c

                lax.fori_loop(q0, SLOTS, clear, 0)
                row = own + ROWS * db

                @pl.when(both(row >= 0, ROWS * db < ROWS + own))
                def _():
                    x_all[:, pl.ds(pl.multiple_of(base + row, 8), ROWS), :] = zf

    @pl.when(is_w)
    def _():
        @pl.when(sw >= 1)
        def _():
            forward(4)

        forward(8)

        @pl.when(sw >= 1)
        def _():
            forward(5)

        forward(9)
        wait_forwarded(8)
        look_up_slots(8, 9)

        @pl.when(sw >= 1)
        def _():
            wait_forwarded(4)
            look_up_slots(4, 5)
            forward(6)

        forward(10)
        wait_forwarded(9)

        @pl.when(sw >= 1)
        def _():
            wait_forwarded(5)
            look_up_slots(5, 6)
            forward(7)

            @pl.when(sw == 3)
            def _():
                wait_sent(4, 5, 6, 7)
                forward(0, 1, 2, 3)

        @pl.when(sw == 0)
        def _():
            for g in range(6):
                jj = 2 * b - 2 + g

                @pl.when(both(jj >= 0, jj < 2 * BLOCKS, g != 3))
                def _():
                    dst = x_all.at[:, pl.ds(X_BASE[16] + HALF * g, HALF), :]
                    remote(surf_block, dst, surf_send.at[0], surf_recv.at[g], (d, jj)).wait_recv()

            self_surf().wait()

            @pl.when(p >= 2)
            def _():
                top = slice(X_BASE[16], X_BASE[17])
                x_all[1, top, :] = -x_all[1, top, :]

            apply(16)
            apply(17)

        look_up_slots(9, 10)
        wait_forwarded(10)
        look_up_slots(10, 11)

        @pl.when(sw == 0)
        def _():
            for i in range(18, 22):
                apply(i)

        @pl.when(sw >= 1)
        def _():
            wait_forwarded(6, 7)
            look_up_slots(6, 8)

        wait_own(SLOTS - 1)
        wait_forwarded(SLOTS - 1)
        look_up(SLOTS - 1, 4)

        @pl.when(sw == 3)
        def _():
            wait_forwarded(0, 1, 2, 3)
            look_up_slots(0, 4)

        @pl.when(is_later)
        def _():
            base, own = x_row(i0)
            for db, on, target in stage_targets(sw - 1, is_later):

                @pl.when(on)
                def _():
                    dst = x_all.at[:, pl.ds(pl.multiple_of(base + own + ROWS * db, 8), ROWS), :]
                    remote(dst, dst, hop_send.at[0], hop_recv.at[db + 3], target).wait_recv()

        def slab(q):
            apply(2 * q)
            apply(2 * q + 1)

            @pl.when(sw == 3)
            def _():
                if q >= 4:
                    wait_images(q - 4)
                send_images(q, 2 * q + 2)

        @pl.when(sw == 3)
        def _():
            for q in range(4):
                slab(q)

        @pl.when(sw >= 1)
        def _():
            for q in range(4, SLOTS - 1):
                slab(q)

        slab(SLOTS - 1)

        @pl.when(is_earlier)
        def _():
            words = jnp.int32(0)
            for db, on, target in stage_targets(sw + 1, is_earlier):
                words += jnp.where(on, 1, 0)
            pl.semaphore_wait(hello, words)
            for db, on, target in stage_targets(sw + 1, is_earlier):

                @pl.when(on)
                def _():
                    hop_copy(db, target).start()

            def slot(q, c):
                @pl.when(q - 4 >= q0)
                def _():
                    wait_images(q - 4)

                send_images(q, 2 * q + 2)
                return c

            lax.fori_loop(q0, SLOTS, slot, 0)

    for f in range(2):
        def wait_image(on, dst, recv):
            @pl.when(on)
            def _():
                remote(dst, dst, im_send.at[0, 0], recv, (d, j + 1 - 2 * core)).wait_recv()

        wait_image(other(worker(so, f, bj)), out_s.at[f], ims_recv.at[f])
        wait_image(other(worker(so, 2 + f, bj)), out_r.at[f, :, pl.ds(pl.multiple_of(8 - 8 * core, 8), 24), :],
                   imr_recv.at[f, 0])
        wait_image(inside(edge_block), out_r.at[f, :, pl.ds(pl.multiple_of(24 * core, 8), 8), :], imr_recv.at[f, 1])

    @pl.when(at_edge)
    def _():
        zero_copy().wait()

    for pp in range(4):

        @pl.when(other(worker(so, pp, bj)))
        def _():
            bin_copy(pp).wait_send()

    @pl.when(edge_on)
    def _():
        for pp in range(4):
            edge_copy(pp).wait_send()

    @pl.when(is_surf)
    def _():
        for db, on, target in surf_targets():

            @pl.when(both(on, other(target)))
            def _():
                surf_copy(db, target).wait_send()

    @pl.when(is_w)
    def _():
        @pl.when(sw == 3)
        def _():
            wait_sent(0, 1, 2, 3)

        @pl.when(both(sw >= 1, sw <= 2))
        def _():
            wait_sent(4, 5, 6, 7)

        wait_sent(8, 9, 10)

        @pl.when(is_earlier)
        def _():
            for db, on, target in stage_targets(sw + 1, is_earlier):

                @pl.when(on)
                def _():
                    hop_copy(db, target).wait_send()

        def slot(q, c):
            wait_images(q)
            return c

        lax.fori_loop(SLOTS - 4, SLOTS, slot, 0)


def image_kernel(offsets, s_ref, r_ref, out_ref):
    lane = lax.broadcasted_iota(jnp.int32, (HALF, 128), 1)
    for h in range(out_ref.shape[1]):
        hy, hx = offsets[0, h], offsets[1, h]
        total = None
        for f in range(2):
            for part in range(2):
                moved = r_ref[f, part, pl.ds(OFF_Y + hy, HALF), :]
                moved = pltpu.roll(moved, lax.rem(128 - hx, 128), 1)
                term = s_ref[f, part] * moved
                total = term if total is None else total + term if part == 0 else total - term
        valid = both(lane + hx >= 0, lane + hx < 128)
        out_ref[0, h] = jnp.where(valid, total, 0.0)


def shards(surface_fields, stencil_table, velocity_bins, offset_list):
    vmem = pl.BlockSpec(memory_space=pltpu.VMEM)
    hbm = pl.BlockSpec(memory_space=pl.ANY)
    f32 = jnp.float32
    dma = pltpu.SemaphoreType.DMA
    source, receiver = pl.pallas_call(
        chain_kernel,
        out_shape=(jax.ShapeDtypeStruct((2, 2, 16, 128), f32), jax.ShapeDtypeStruct((2, 2, 32, 128), f32)),
        in_specs=[hbm] * 3,
        out_specs=(hbm, hbm),
        scratch_shapes=[
            pltpu.VMEM((2, sum(X_ROWS), 128), f32),
            pltpu.VMEM((2 * len(TAPS), 8 * (UNIT_BASE[LEVELS] + GATHER), 128), f32),
            pltpu.VMEM((SLOTS, 2, BIN_ROWS, 128), jnp.int32),
            pltpu.VMEM((2 * len(TAPS), 8, 128), f32),
            pltpu.VMEM(stencil_table.shape, f32),
            pltpu.VMEM((2, 2, OFF_Y, 128), f32),
            dma, dma((3,)), dma,
            dma((4,)), dma((SLOTS,)), dma((4,)), dma((30,)), dma((SLOTS, 2)),
            dma((3,)), dma((6,)), dma((7,)), dma((7,)),
            dma((4, 4)), dma((2,)), dma((2, 2)), pltpu.SemaphoreType.REGULAR,
        ],
        compiler_params=pltpu.CompilerParams(
            collective_id=0, has_side_effects=True, vmem_limit_bytes=56 * 2**20),
    )(surface_fields, stencil_table, velocity_bins)
    return pl.pallas_call(
        image_kernel,
        out_shape=jax.ShapeDtypeStruct((1, offset_list.shape[0], HALF, 128), f32),
        in_specs=[pl.BlockSpec(memory_space=pltpu.SMEM), vmem, vmem],
        out_specs=vmem,
    )(offset_list.T, source, receiver)


def solution(mesh):
    return jax.shard_map(
        shards,
        mesh=mesh,
        in_specs=(P(None, None, None, "xline", None), P(), P("depth", None, "xline", None), P()),
        out_specs=P("depth", None, "xline", None),
        check_vma=False,
    )
```

```python
import jax
import jax.numpy as jnp
from jax import lax
from jax.experimental import pallas as pl
from jax.experimental.pallas import tpu as pltpu
from jax.sharding import PartitionSpec as P

MESH = pl.DeviceIdType.MESH

OFF_Y = 8
TAPS = ((0, 0), (-4, 0), (-3, 0), (-2, 0), (-1, 0), (1, 0), (2, 0), (3, 0), (4, 0), (0, -2), (0, -1), (0, 1), (0, 2))
REACH = 4

LEVELS = 24
SLOTS = LEVELS // 2
ROWS = 32
BLOCKS = 8
HALF = 16
GRID = 256

UNITS = [ROWS // 8 + LEVELS - 1 - i for i in range(LEVELS)]
UNIT_BASE = [sum(UNITS[:i]) for i in range(LEVELS + 1)]
X_ROWS = [ROWS + 2 * REACH * (LEVELS - m) for m in range(LEVELS + 1)]
X_BASE = [sum(X_ROWS[:m]) for m in range(LEVELS + 1)]
BIN_PAD = REACH * LEVELS
BIN_ROWS = ROWS + 2 * BIN_PAD
GATHER = 6
CHUNK = 7


def pick(s, *values):
    return jnp.where(s == 0, values[0], jnp.where(s == 1, values[1], jnp.where(s == 2, values[2], values[3])))


def stage_of(d):
    return jnp.where(d < 4, 0, jnp.where(d < 12, 1, jnp.where(d < 20, 2, 3)))


def stage_end(s):
    return pick(s, 4, 12, 20, 32)


def first_level(s):
    return pick(s, 16, 8, 8, 0)


def worker(s, p, b):
    plane = jnp.where(s <= 1, p >> 1, 7 - 5 * (p >> 1))
    return 4 * plane + (p & 1), 2 * b + pick(s, 1, 0, 0, 1)


def halo(level):
    return REACH * (LEVELS - 1 - level)


def sent_halo(q):
    return -(-halo(2 * q) // 8) * 8


def both(*conditions):
    out = conditions[0]
    for c in conditions[1:]:
        out = jnp.logical_and(out, c)
    return out


def chain_kernel(
    surf_ref, tab_hbm, bins_ref, out_s, out_r,
    x_all, coef, bins_all, tab8, tab_ref, zero_rows,
    tab_sem, self_sem, zero_sem, bin_send, bin_recv, edge_send, fwd_send, fwd_recv, surf_send, surf_recv, hop_send, hop_recv,
    im_send, ims_recv, imr_recv, hello,
):
    d, j = lax.axis_index("depth"), lax.axis_index("xline")
    y, zh, bj, core = d >> 2, d & 3, j >> 1, j & 1
    so = stage_of(d)
    qo = d - stage_end(so) + SLOTS
    sw = jnp.where(y <= 1, 1 - core, 2 + core)
    yw = jnp.where(both(y >= 1, y <= 2), 1, 0)
    is_w = both(zh <= 1, jnp.where(y == 7, True, y <= 2))
    p, b = 2 * yw + zh, bj
    i0 = first_level(sw)
    q0 = i0 >> 1
    ew = stage_end(sw)
    is_surf = both(y <= 1, zh <= 1)
    self_slot = both(so == sw, is_w)

    def me(target):
        return both(target[0] == d, target[1] == j)

    def other(target):
        return jnp.logical_not(me(target))

    def inside(block):
        return both(block >= 0, block < BLOCKS)

    def remote(src, dst, send, recv, target):
        return pltpu.make_async_remote_copy(
            src_ref=src, dst_ref=dst, send_sem=send, recv_sem=recv, device_id=target, device_id_type=MESH)

    def surf_targets():
        for db in (0, -1, 1):
            bb = bj + db
            yield db, both(is_surf, inside(bb)), (d, 2 * bb + 1)

    def stage_targets(s, on):
        for db in (0, -1, 1, -2, 2, -3, 3):
            bb = b + db
            near = True if abs(db) <= 2 else jnp.maximum(s, sw) == 3
            yield db, both(on, inside(bb), near), worker(s, p, bb)

    SIDES = (-1, 1, -2, 2, -3, 3)

    def beside():
        for e, db in enumerate(SIDES):
            near = sw >= (0, 1, 3)[abs(db) - 1]
            yield e, db, both(is_w, inside(b + db), near), worker(sw, p, b + db)

    is_later = both(is_w, sw >= 1)
    is_earlier = both(is_w, sw <= 2)
    edge_block = bj + 2 * core - 1
    edge_on = both(qo == SLOTS - 1, inside(edge_block))

    barrier = pltpu.get_barrier_semaphore()

    def greet(target):
        pl.semaphore_signal(barrier, inc=1, device_id=target, device_id_type=MESH)

    tab_copy = pltpu.make_async_copy(tab_hbm, tab_ref, tab_sem)

    @pl.when(is_w)
    def _():
        tab_copy.start()

        @pl.when(sw == 0)
        def _():
            for g in range(6):
                source = (d, 2 * b - 2 + g)

                @pl.when(both(source[1] >= 0, source[1] < 2 * BLOCKS, g != 3))
                def _():
                    greet(source)

        def slot(q, c):
            mine = both(self_slot, q == qo)

            @pl.when(jnp.logical_not(both(mine, core == 0)))
            def _():
                greet((ew - SLOTS + q, 2 * b))

            @pl.when(jnp.logical_not(both(mine, core == 1)))
            def _():
                greet((ew - SLOTS + q, 2 * b + 1))

            return c

        lax.fori_loop(q0, SLOTS, slot, 0)
        for db, on, target in stage_targets(sw + 1, is_earlier):

            @pl.when(on)
            def _():
                greet(target)

        for e, db, on, target in beside():

            @pl.when(on)
            def _():
                greet(target)

        @pl.when(b > 0)
        def _():
            greet((ew - 1, 2 * b - 1))

        @pl.when(b < BLOCKS - 1)
        def _():
            greet((ew - 1, 2 * b + 2))

    zero_rows[...] = jnp.zeros((2, 2, OFF_Y, 128), jnp.float32)

    def zero_copy():
        return pltpu.make_async_copy(
            zero_rows, out_r.at[:, :, pl.ds(pl.multiple_of(24 * core, 8), OFF_Y), :], zero_sem)

    at_edge = jnp.logical_not(inside(edge_block))

    @pl.when(at_edge)
    def _():
        zero_copy().start()

    def x_row(level):
        base = level * (ROWS + 2 * REACH * LEVELS) - REACH * level * (level - 1)
        return pl.multiple_of(base, 8), pl.multiple_of(REACH * (LEVELS - level), 8)

    count = jnp.int32(0)
    for pp in range(4):
        count += jnp.where(other(worker(so, pp, bj)), 1, 0)
    count += jnp.where(edge_on, 4, 0)
    for db, on, target in surf_targets():
        count += jnp.where(both(on, other(target)), 1, 0)
    for db, on, target in stage_targets(sw - 1, is_later):
        count += jnp.where(on, 1, 0)
    for e, db, on, target in beside():
        count += jnp.where(on, 1, 0)
    pl.semaphore_wait(barrier, count)

    own_rows = pl.multiple_of(BIN_PAD + HALF * core, HALF)

    def bin_copy(pp):
        return remote(bins_ref.at[0], bins_all.at[qo, :, pl.ds(own_rows, HALF), :],
                      bin_send.at[pp], bin_recv.at[qo], worker(so, pp, bj))

    def edge_copy(pp):
        start = pl.multiple_of(8 * core, 8)
        to = pl.multiple_of(jnp.where(core == 1, BIN_PAD - 8, BIN_PAD + ROWS), 8)
        return remote(bins_ref.at[0, :, pl.ds(start, 8), :], bins_all.at[SLOTS - 1, :, pl.ds(to, 8), :],
                      edge_send.at[pp], fwd_recv.at[SLOTS - 1, 1 - core], worker(so, pp, edge_block))

    surf_block = surf_ref.at[jnp.minimum(y, 1), :, jnp.minimum(zh, 1)]

    def surf_row():
        return X_BASE[16] + 32 + HALF * core

    def surf_copy(db, target):
        row = pl.multiple_of(surf_row() - ROWS * db, 8)
        return remote(surf_block, x_all.at[:, pl.ds(row, HALF), :], surf_send.at[db + 1],
                      surf_recv.at[core - 2 * db + 2], target)

    def self_bins():
        return pltpu.make_async_copy(
            bins_ref.at[0], bins_all.at[qo, :, pl.ds(own_rows, HALF), :], self_sem.at[0])

    def self_surf():
        return pltpu.make_async_copy(
            surf_block, x_all.at[:, pl.ds(X_BASE[16] + 32 + HALF, HALF), :], self_sem.at[1])

    for pp in range(4):
        target = worker(so, pp, bj)

        @pl.when(other(target))
        def _():
            bin_copy(pp).start()

        @pl.when(me(target))
        def _():
            self_bins().start()

    @pl.when(edge_on)
    def _():
        for pp in range(4):
            edge_copy(pp).start()

    @pl.when(is_surf)
    def _():
        for db, on, target in surf_targets():

            @pl.when(both(on, other(target)))
            def _():
                surf_copy(db, target).start()

            @pl.when(both(on, me(target)))
            def _():
                self_surf().start()

    @pl.when(is_later)
    def _():
        for db, on, target in stage_targets(sw - 1, is_later):

            @pl.when(on)
            def _():
                pl.semaphore_signal(hello, inc=1, device_id=target, device_id_type=MESH)

    def forwards(q):
        for e, db, on, target in beside():
            rows = min(ROWS, sent_halo(q) - ROWS * (abs(db) - 1))
            if rows > 0:
                start = BIN_PAD if db < 0 else BIN_PAD + ROWS - rows
                src = bins_all.at[q, :, start : start + rows, :]
                to = start - ROWS * db
                dst = bins_all.at[q, :, to : to + rows, :]
                send = fwd_send.at[(6 * q if q < 4 else 24 + 4 * (q - 4) if q < 8 else 40 + 2 * (q - 8)) + e]
                yield on, remote(src, dst, send, fwd_recv.at[q, 0 if db > 0 else 1], target)

    def wait_sent(*slots):
        for q in slots:
            for on, copy in forwards(q):

                @pl.when(on)
                def _():
                    copy.wait_send()

    def wait_own(q):
        here = both(self_slot, q == qo)

        @pl.when(jnp.logical_not(here))
        def _():
            dst = bins_all.at[q, :, BIN_PAD : BIN_PAD + ROWS, :]
            remote(dst, dst, bin_send.at[0], bin_recv.at[q], (ew - SLOTS + q, 2 * b)).wait_recv()

        @pl.when(here)
        def _():
            dst = bins_all.at[q, :, pl.ds(pl.multiple_of(BIN_PAD + HALF * (1 - core), HALF), HALF), :]
            remote(dst, dst, bin_send.at[0], bin_recv.at[q], (d, j + 1 - 2 * core)).wait_recv()
            self_bins().wait()

    def forward(*slots):
        for q in slots:
            wait_own(q)
            for on, copy in forwards(q):

                @pl.when(on)
                def _():
                    copy.start()

    def wait_forwarded(*slots):
        for q in slots:
            rows_all = sent_halo(q)
            deepest = -(-rows_all // ROWS)
            for side in range(2):
                there = b if side == 0 else BLOCKS - 1 - b
                for k in range(1, deepest + 1):
                    rows = min(rows_all, ROWS * k)
                    start = BIN_PAD - rows if side == 0 else BIN_PAD + ROWS
                    dst = bins_all.at[q, :, start : start + rows, :]

                    @pl.when(there >= k if k == deepest else there == k)
                    def _():
                        remote(dst, dst, bin_send.at[0], fwd_recv.at[q, side], (d, j + 1 - 2 * core)).wait_recv()

    def hop_copy(db, target):
        base, own = x_row(first_level(sw + 1))
        row = pl.multiple_of(base + own - ROWS * db, 8)
        return remote(x_all.at[:, pl.ds(X_BASE[LEVELS], ROWS), :], x_all.at[:, pl.ds(row, ROWS), :],
                      hop_send.at[db + 3], hop_recv.at[3 - db], target)

    def source_images(q, row):
        dd, f = ew - SLOTS + q, (p & 1)
        for half in range(2):
            yield half, remote(x_all.at[:, pl.ds(pl.multiple_of(row + HALF * half, 8), HALF), :], out_s.at[f],
                               im_send.at[q, half], ims_recv.at[f], (dd, 2 * b + half))

    def receiver_images(q, row):
        dd, f = ew - SLOTS + q, (p & 1)
        for half in range(2):
            yield half, remote(x_all.at[:, pl.ds(pl.multiple_of(row + 8 * half, 8), 24), :],
                               out_r.at[f, :, pl.ds(8 - 8 * half, 24), :],
                               im_send.at[q, half], imr_recv.at[f, 0], (dd, 2 * b + half))

    def edge_images(q, row):
        dd, f = ew - SLOTS + q, (p & 1)
        for half in range(2):
            on = b > 0 if half == 0 else b < BLOCKS - 1
            yield on, remote(x_all.at[:, pl.ds(pl.multiple_of(row + 24 * half, 8), 8), :],
                             out_r.at[f, :, pl.ds(24 - 24 * half, 8), :],
                             im_send.at[q, 2 + half], imr_recv.at[f, 1], (dd, 2 * b - 1 + 3 * half))

    def send_images(q, level):
        base, own = x_row(level) if not isinstance(level, int) else (X_BASE[level], REACH * (LEVELS - level))
        row = base + own
        mine = both(self_slot, q == qo)

        def pair(images, local):
            for half, copy in images(q, row):
                here = both(mine, core == half)

                @pl.when(jnp.logical_not(here))
                def _():
                    copy.start()

                @pl.when(here)
                def _():
                    local(half)

        def local_source(half):
            copy = pltpu.make_async_copy(
                x_all.at[:, pl.ds(pl.multiple_of(row + HALF * half, 8), HALF), :], out_s.at[(p & 1)], self_sem.at[2])
            copy.start()
            copy.wait()

        def local_receiver(half):
            copy = pltpu.make_async_copy(
                x_all.at[:, pl.ds(pl.multiple_of(row + 8 * half, 8), 24), :],
                out_r.at[(p & 1), :, pl.ds(8 - 8 * half, 24), :], self_sem.at[2])
            copy.start()
            copy.wait()

        @pl.when(p < 2)
        def _():
            pair(source_images, local_source)

        @pl.when(p >= 2)
        def _():
            pair(receiver_images, local_receiver)
            for on, copy in edge_images(q, row):

                @pl.when(on)
                def _():
                    copy.start()

    def wait_images(q):
        base, own = x_row(2 * q + 2)
        mine = both(self_slot, q == qo)

        def pair(images):
            for half, copy in images(q, base + own):

                @pl.when(jnp.logical_not(both(mine, core == half)))
                def _():
                    copy.wait_send()

        @pl.when(p < 2)
        def _():
            pair(source_images)

        @pl.when(p >= 2)
        def _():
            pair(receiver_images)
            for on, copy in edge_images(q, base + own):

                @pl.when(on)
                def _():
                    copy.wait_send()

    def apply(i):
        n, base, out = UNITS[i], X_BASE[i], X_BASE[i + 1]
        pieces = -(-n // CHUNK)
        cuts = [n * k // pieces for k in range(pieces + 1)]
        for u0, u1 in zip(cuts, cuts[1:]):
            r, rows = 8 * u0, 8 * (u1 - u0)
            unit = 8 * (UNIT_BASE[i] + u0)
            rr = ii = ri = ir = None
            for t, (dy, dx) in enumerate(TAPS):
                cr, ci = coef[2 * t, unit : unit + rows, :], coef[2 * t + 1, unit : unit + rows, :]
                at = base + r + REACH + dy
                fr, fi = x_all[0, at : at + rows, :], x_all[1, at : at + rows, :]
                if dx != 0:
                    fr, fi = pltpu.roll(fr, (-dx) % 128, 1), pltpu.roll(fi, (-dx) % 128, 1)
                if rr is None:
                    rr, ii, ri, ir = cr * fr, ci * fi, cr * fi, ci * fr
                else:
                    rr, ii, ri, ir = rr + cr * fr, ii + ci * fi, ri + cr * fi, ir + ci * fr
            x_all[0, out + r : out + r + rows, :] = rr - ii
            x_all[1, out + r : out + r + rows, :] = ri + ir

    def look_up(q, size):
        lane = lax.broadcasted_iota(jnp.int32, (8, 128), 1)
        sub = lax.broadcasted_iota(jnp.int32, (8, 128), 0)
        for step in range(2):
            i = 2 * q + step
            n = ROWS // 8 + LEVELS - 1 - i
            first = (ROWS // 8 + LEVELS - 1) * i - i * (i - 1) // 2

            def group(k, c):
                u = jnp.minimum(k * size, n - size)
                for e in range(size):
                    row = REACH + REACH * i + 8 * (u + e)
                    index = bins_all[q, step, pl.ds(row, 8), :]
                    line = ROWS * b - REACH * (LEVELS - 1 - i) + 8 * (u + e) + sub
                    valid = both(line >= 0, line < GRID)
                    to = pl.multiple_of(8 * (first + u + e), 8)
                    for t, (dy, dx) in enumerate(TAPS):
                        keep = valid
                        if dx > 0:
                            keep = both(valid, lane < 128 - dx)
                        elif dx < 0:
                            keep = both(valid, lane >= -dx)
                        for part in range(2):
                            value = jnp.take_along_axis(
                                tab8[2 * t + part], index, axis=1, mode="promise_in_bounds")
                            coef[2 * t + part, pl.ds(to, 8), :] = jnp.where(keep, value, 0.0)
                return c

            lax.fori_loop(0, (n + size - 1) // size, group, 0)

    def look_up_slots(start, end):
        def slot(q, c):
            look_up(q, GATHER)
            return c

        lax.fori_loop(start, end, slot, 0)

    @pl.when(is_w)
    def _():
        f = (p & 1)
        tab_copy.wait()
        for t in range(2 * len(TAPS)):
            tab8[t] = jnp.broadcast_to(tab_ref[t // 2, t % 2, pl.ds(f, 1), :], (8, 128))
        base, own = x_row(i0)
        zf = jnp.zeros((2, ROWS, 128), jnp.float32)
        zi = jnp.zeros((2, ROWS, 128), jnp.int32)
        for db in SIDES:

            @pl.when(jnp.logical_not(inside(b + db)))
            def _():
                def clear(q, c):
                    bins_all[q, :, pl.ds(BIN_PAD + ROWS * db, ROWS), :] = zi
                    return c

                lax.fori_loop(q0, SLOTS, clear, 0)
                row = own + ROWS * db

                @pl.when(sw >= (0, 1, 3)[abs(db) - 1])
                def _():
                    x_all[:, pl.ds(pl.multiple_of(base + row, 8), ROWS), :] = zf

    @pl.when(is_w)
    def _():
        def look_up_last():
            wait_own(SLOTS - 1)
            wait_forwarded(SLOTS - 1)
            look_up(SLOTS - 1, 4)

        @pl.when(sw == 0)
        def _():
            forward(8, 9)
            wait_forwarded(8)
            look_up(8, GATHER)

            for g in range(6):
                jj = 2 * b - 2 + g

                @pl.when(both(jj >= 0, jj < 2 * BLOCKS, g != 3))
                def _():
                    dst = x_all.at[:, pl.ds(X_BASE[16] + HALF * g, HALF), :]
                    remote(surf_block, dst, surf_send.at[0], surf_recv.at[g], (d, jj)).wait_recv()

            self_surf().wait()

            @pl.when(p >= 2)
            def _():
                top = slice(X_BASE[16], X_BASE[17])
                x_all[1, top, :] = -x_all[1, top, :]

            apply(16)
            apply(17)
            forward(10)
            wait_forwarded(9)
            look_up(9, GATHER)
            apply(18)
            apply(19)
            wait_forwarded(10)
            look_up(10, GATHER)
            apply(20)
            apply(21)
            look_up_last()

        @pl.when(sw >= 1)
        def _():
            forward(4, 8, 5, 9)

            @pl.when(sw == 3)
            def _():
                forward(0, 1)

            wait_forwarded(4)
            look_up(4, 9)
            wait_forwarded(8)
            look_up(8, GATHER)
            forward(6, 10)

            @pl.when(sw == 3)
            def _():
                forward(2)

            wait_forwarded(5)
            look_up(5, 9)
            forward(7)

            @pl.when(sw == 3)
            def _():
                forward(3)

            wait_forwarded(6)
            look_up(6, 9)
            wait_forwarded(9, 10)
            look_up_slots(9, 11)
            wait_forwarded(7)
            look_up(7, GATHER)
            look_up_last()

            @pl.when(sw == 3)
            def _():
                wait_forwarded(0, 1, 2, 3)
                look_up(3, 12)
                look_up(2, 12)
                look_up(1, 9)
                look_up(0, 9)

        @pl.when(is_later)
        def _():
            base, own = x_row(i0)
            for db, on, target in stage_targets(sw - 1, is_later):

                @pl.when(on)
                def _():
                    dst = x_all.at[:, pl.ds(pl.multiple_of(base + own + ROWS * db, 8), ROWS), :]
                    remote(dst, dst, hop_send.at[0], hop_recv.at[db + 3], target).wait_recv()

        def slab(q):
            apply(2 * q)
            apply(2 * q + 1)

            @pl.when(sw == 3)
            def _():
                send_images(q, 2 * q + 2)

        def slabs(on, start, end):
            @pl.when(on)
            def _():
                for q in range(start, end):
                    slab(q)

        slabs(sw == 3, 0, 4)
        slabs(sw >= 1, 4, SLOTS - 1)
        slab(SLOTS - 1)

        @pl.when(is_earlier)
        def _():
            words = jnp.int32(0)
            for db, on, target in stage_targets(sw + 1, is_earlier):
                words += jnp.where(on, 1, 0)
            pl.semaphore_wait(hello, words)
            for db, on, target in stage_targets(sw + 1, is_earlier):

                @pl.when(on)
                def _():
                    hop_copy(db, target).start()

            def slot(q, c):
                send_images(q, 2 * q + 2)
                return c

            lax.fori_loop(q0, SLOTS, slot, 0)

    for f in range(2):
        def wait_image(on, dst, recv):
            @pl.when(on)
            def _():
                remote(dst, dst, im_send.at[0, 0], recv, (d, j + 1 - 2 * core)).wait_recv()

        wait_image(other(worker(so, f, bj)), out_s.at[f], ims_recv.at[f])
        wait_image(other(worker(so, 2 + f, bj)), out_r.at[f, :, pl.ds(pl.multiple_of(8 - 8 * core, 8), 24), :],
                   imr_recv.at[f, 0])
        wait_image(inside(edge_block), out_r.at[f, :, pl.ds(pl.multiple_of(24 * core, 8), 8), :], imr_recv.at[f, 1])

    @pl.when(at_edge)
    def _():
        zero_copy().wait()

    for pp in range(4):

        @pl.when(other(worker(so, pp, bj)))
        def _():
            bin_copy(pp).wait_send()

    @pl.when(edge_on)
    def _():
        for pp in range(4):
            edge_copy(pp).wait_send()

    @pl.when(is_surf)
    def _():
        for db, on, target in surf_targets():

            @pl.when(both(on, other(target)))
            def _():
                surf_copy(db, target).wait_send()

    @pl.when(is_w)
    def _():
        @pl.when(sw == 3)
        def _():
            wait_sent(0, 1, 2, 3)

        @pl.when(sw >= 1)
        def _():
            wait_sent(4, 5, 6, 7)

        wait_sent(8, 9, 10)

        @pl.when(is_earlier)
        def _():
            for db, on, target in stage_targets(sw + 1, is_earlier):

                @pl.when(on)
                def _():
                    hop_copy(db, target).wait_send()

        def slot(q, c):
            wait_images(q)
            return c

        lax.fori_loop(q0, SLOTS, slot, 0)


def image_kernel(offsets, s_ref, r_ref, out_ref):
    lane = lax.broadcasted_iota(jnp.int32, (HALF, 128), 1)
    for h in range(out_ref.shape[1]):
        hy, hx = offsets[0, h], offsets[1, h]
        total = None
        for f in range(2):
            for part in range(2):
                moved = r_ref[f, part, pl.ds(OFF_Y + hy, HALF), :]
                moved = pltpu.roll(moved, lax.rem(128 - hx, 128), 1)
                term = s_ref[f, part] * moved
                total = term if total is None else total + term if part == 0 else total - term
        valid = both(lane + hx >= 0, lane + hx < 128)
        out_ref[0, h] = jnp.where(valid, total, 0.0)


def shards(surface_fields, stencil_table, velocity_bins, offset_list):
    vmem = pl.BlockSpec(memory_space=pltpu.VMEM)
    hbm = pl.BlockSpec(memory_space=pl.ANY)
    f32 = jnp.float32
    dma = pltpu.SemaphoreType.DMA
    source, receiver = pl.pallas_call(
        chain_kernel,
        out_shape=(jax.ShapeDtypeStruct((2, 2, 16, 128), f32), jax.ShapeDtypeStruct((2, 2, 32, 128), f32)),
        in_specs=[hbm] * 3,
        out_specs=(hbm, hbm),
        scratch_shapes=[
            pltpu.VMEM((2, sum(X_ROWS), 128), f32),
            pltpu.VMEM((2 * len(TAPS), 8 * (UNIT_BASE[LEVELS] + GATHER), 128), f32),
            pltpu.VMEM((SLOTS, 2, BIN_ROWS, 128), jnp.int32),
            pltpu.VMEM((2 * len(TAPS), 8, 128), f32),
            pltpu.VMEM(stencil_table.shape, f32),
            pltpu.VMEM((2, 2, OFF_Y, 128), f32),
            dma, dma((3,)), dma,
            dma((4,)), dma((SLOTS,)), dma((4,)), dma((46,)), dma((SLOTS, 2)),
            dma((3,)), dma((6,)), dma((7,)), dma((7,)),
            dma((SLOTS, 4)), dma((2,)), dma((2, 2)), pltpu.SemaphoreType.REGULAR,
        ],
        compiler_params=pltpu.CompilerParams(
            collective_id=0, has_side_effects=True, vmem_limit_bytes=56 * 2**20),
    )(surface_fields, stencil_table, velocity_bins)
    return pl.pallas_call(
        image_kernel,
        out_shape=jax.ShapeDtypeStruct((1, offset_list.shape[0], HALF, 128), f32),
        in_specs=[pl.BlockSpec(memory_space=pltpu.SMEM), vmem, vmem],
        out_specs=vmem,
    )(offset_list.T, source, receiver)


def solution(mesh):
    return jax.shard_map(
        shards,
        mesh=mesh,
        in_specs=(P(None, None, None, "xline", None), P(), P("depth", None, "xline", None), P()),
        out_specs=P("depth", None, "xline", None),
        check_vma=False,
    )
```
